1024 devices in a mesh: group: 8 (over y), node: 64 (over x, z), tp: 2 (over core).
Axes of the slice: x: 4, y: 8, z: 16, core: 2. Of those that a mesh axis runs over, the one named last changes fastest.
Arguments:
- out_grad: bfloat16 [64, 64, 3584], P('node', 'group', 'tp'), may hold values from -6 to 6
- expert_ids: int32 [64, 64, 8], P('node'), may hold values from 0 to 127, all different within a row; in each aligned block of 64 rows (0 to 63, 64 to 127, ..., all dimensions but the last counted through in order) at most 8 rows name the same one
- gate_scores: bfloat16 [64, 64, 8], P('node'), may hold values from 0.099609375 to 0.59765625
- saved_gate: bfloat16 [512, 64, 8, 256], P(('group', 'node')), may hold values from -6 to 6
- saved_up: bfloat16 [512, 64, 8, 256], P(('group', 'node')), may hold values from -6 to 6
- w_gate: bfloat16 [512, 3584, 256], P(('group', 'node'), 'tp'), may hold values from -0.09375 to 0.09375
- w_up: bfloat16 [512, 3584, 256], P(('group', 'node'), 'tp'), may hold values from -0.09375 to 0.09375
- w_down: bfloat16 [512, 256, 3584], P(('group', 'node'), None, 'tp'), may hold values from -0.1875 to 0.1875
Outputs:
- input_grad: bfloat16 [64, 64, 3584], P('node', 'group', 'tp')
The draws below stay inside these ranges and needn't reach their ends.
Inputs may be any that keep to these rules, and one draw needn't show every extreme that they name: Each row names 8 different experts; among the rows expert_ids[n, :, :] of one n no expert is named more than 8 times.
All inputs are finite; a program needn't handle non-finite values.
Results may differ from the reference program's by a relative error of at most 0.009.
Values may be sent and summed in bfloat16 or wider, within the bound.
A program may use at most 32 MiB of HBM per device.

```python
import math
import jax
import jax.numpy as jnp
import numpy as np
from jax import lax

D = 3584
FF = 1024
TOPK = 8
NPE = 4
EXPERTS = 128
HID = 256
ROWS = 64
MOST = 8
N_GROUP = 8
N_NODE = 64


def block_scale(own_key, shape, pieces, least, high):
    def one(dim, parts):
        steps = jax.random.uniform(jax.random.fold_in(jax.random.fold_in(own_key, 6), dim), (parts,), jnp.float32, least / len(pieces), high / len(pieces))
        return jnp.repeat(jnp.exp(steps), shape[dim] // parts).reshape((-1,) + (1,) * (len(shape) - dim - 1))

    gain = one(*pieces[0])
    for cut in pieces[1:]:
        gain = gain * one(*cut)
    return gain


def deal_out(rng, own, number, rows, count, top, bound, lean):
    ranking = jax.random.permutation(rng, count)
    crowded, ordinary = shares(count, rows * top, bound, lean, True), shares(count, rows * top, bound, lean, False)
    places = jnp.arange(count)

    def named(lengths, turn):
        used = int((lengths > 0).sum())
        fixed = max(1, used // 4)
        moved = fixed + (places - fixed + turn * (used - fixed)) % max(1, count - fixed)
        return jnp.zeros((count,), jnp.int32).at[ranking[jnp.where(places < fixed, places, moved)]].set(jnp.asarray(lengths, jnp.int32))

    lengths = jnp.where(number % 4 == 0, named(crowded, number // 4), named(ordinary, number - number // 4 - 1))
    mixed = jax.random.permutation(jax.random.fold_in(own, 3), count)
    source_of, taker = mixed[0:count // 2 * 2:2], mixed[1:count // 2 * 2:2]
    margin = jnp.minimum(lengths[source_of] - 1, bound - lengths[taker]) // 2
    margin = jnp.where((source_of == ranking[0]) | (taker == ranking[0]) | (lengths[taker] == 0), 0, jnp.maximum(margin, 0))
    moved = jax.random.randint(jax.random.fold_in(own, 4), (count // 2,), 0, 1 << 20) % (margin + 1)
    lengths = lengths.at[source_of].add(-moved).at[taker].add(moved)
    members = jnp.searchsorted(jnp.cumsum(lengths), jnp.arange(rows * top), side="right").astype(jnp.int32)
    grid = members.reshape(top, rows).T
    grid = grid[jax.random.permutation(jax.random.fold_in(own, 1), rows)]
    turn = jax.random.randint(jax.random.fold_in(own, 2), (rows, 1), 0, top)
    return jnp.take_along_axis(grid, (jnp.arange(top)[None, :] + turn) % top, axis=1)


def shares(amount, total, most, lean, full):
    loads = [(1 << 20) // math.isqrt(rank ** lean) + 1 for rank in range(1, amount + 1)]
    largest = most if full else min(most, max(-(-total // amount), total * loads[0] // sum(loads)))
    least = 1 if total - largest >= amount - 1 else 0
    given, rest = [largest] + [least] * (amount - 1), total - largest - least * (amount - 1)
    while rest > 0:
        movable = [i for i in range(1, amount) if given[i] < largest] or [i for i in range(1, amount) if given[i] < most]
        pool, left = sum([loads[i] for i in movable]), rest
        for i in movable:
            extra = min(most - given[i], max(1, left * loads[i] // pool), rest)
            given[i] = given[i] + extra
            rest = rest - extra
    return np.array(given)


def centred(stream_key, extent, spread, limit, shards=(), kind=jnp.bfloat16):
    values = jax.random.normal(stream_key, extent, jnp.float32) * spread
    if len(shards) > 0:
        values = block_scale(stream_key, extent, shards, -0.22, 0.18) * values
    return jnp.clip(values, min=-limit, max=limit).astype(kind)


def setup_inputs(seed: int = 0) -> dict:
    seeds = jax.random.split(jax.random.key(seed), 9)
    out_grad = centred(seeds[0], (N_NODE, ROWS, D), 1.0, 6.0, ((0, 64), (1, 8), (2, 2)))
    expert_ids_keys = jax.random.split(jax.random.fold_in(seeds[1], 1), N_NODE * ROWS // ROWS)
    expert_ids_turns = jax.random.permutation(jax.random.fold_in(seeds[1], 3), N_NODE * ROWS // ROWS)
    expert_ids = jax.vmap(lambda own, number: deal_out(jax.random.fold_in(seeds[1], 2), own, number, ROWS, EXPERTS, TOPK, MOST, 2))(expert_ids_keys, expert_ids_turns).reshape((N_NODE, ROWS, TOPK))
    gate_scores = jnp.clip(0.099609375 + 0.49804688 * jax.random.uniform(seeds[2], (N_NODE, ROWS, TOPK), jnp.float32) ** block_scale(seeds[2], (N_NODE, ROWS, TOPK), ((0, 64),), -0.2, 0.2), 0.099609375, 0.59765625).astype(jnp.bfloat16)
    saved_gate = centred(seeds[3], (N_GROUP * N_NODE, N_NODE, MOST, HID), 1.0, 6.0, ((0, 512),))
    saved_up = centred(seeds[4], (N_GROUP * N_NODE, N_NODE, MOST, HID), 1.0, 6.0, ((0, 512),))
    w_gate = centred(seeds[5], (N_GROUP * N_NODE, D, HID), D ** -0.5, 0.09375, ((0, 512), (1, 2)))
    w_up = centred(seeds[6], (N_GROUP * N_NODE, D, HID), D ** -0.5, 0.09375, ((0, 512), (1, 2)))
    w_down = centred(seeds[7], (N_GROUP * N_NODE, HID, D), FF ** -0.5, 0.1875, ((0, 512), (2, 2)))
    return {"out_grad": out_grad, "expert_ids": expert_ids, "gate_scores": gate_scores, "saved_gate": saved_gate, "saved_up": saved_up, "w_gate": w_gate, "w_up": w_up, "w_down": w_down}


def reference(out_grad, expert_ids, gate_scores, saved_gate, saved_up, w_gate, w_up, w_down):
    slots_all = N_NODE * MOST
    gate_w = w_gate.reshape(EXPERTS, NPE, D, HID)
    up_w = w_up.reshape(EXPERTS, NPE, D, HID)
    down_w = w_down.reshape(EXPERTS, NPE, HID, D)
    gate_saved = saved_gate.reshape(EXPERTS, NPE, N_NODE, MOST, HID)
    up_saved = saved_up.reshape(EXPERTS, NPE, N_NODE, MOST, HID)
    scores = gate_scores.astype(jnp.float32)
    grad_wide = out_grad.astype(jnp.float32)
    slot_range = jnp.arange(MOST, dtype=jnp.int32)

    def per_expert(total, expert):
        hits = expert_ids == expert
        pick = jnp.sum(hits.astype(jnp.int32), axis=2)
        weight = jnp.sum(jnp.where(hits, scores, jnp.float32(0.0)), axis=2)
        slot_index = jnp.cumsum(pick, axis=1) - pick
        placing = ((slot_index[:, None, :] == slot_range[None, :, None]) & (pick[:, None, :] > 0)).astype(jnp.float32)
        expert_rows = jnp.einsum("nqr,nrd->nqd", placing, grad_wide, precision=lax.Precision.HIGHEST).astype(jnp.bfloat16)
        slot_weight = jnp.einsum("nqr,nr->nq", placing, weight, precision=lax.Precision.HIGHEST)
        flat_rows = expert_rows.reshape(slots_all, D)
        down_full = down_w[expert].transpose(2, 0, 1).reshape(D, FF)
        hidden_grad = jnp.dot(flat_rows, down_full, preferred_element_type=jnp.float32)
        gate_pre = gate_saved[expert].transpose(1, 2, 0, 3).reshape(slots_all, FF).astype(jnp.float32)
        up_pre = up_saved[expert].transpose(1, 2, 0, 3).reshape(slots_all, FF).astype(jnp.float32)
        scaled = slot_weight.reshape(slots_all, 1) * hidden_grad
        sigmoid_gate = jax.nn.sigmoid(gate_pre)
        gate_grad = (scaled * up_pre * sigmoid_gate * (1.0 + gate_pre * (1.0 - sigmoid_gate))).astype(jnp.bfloat16)
        up_grad = (scaled * gate_pre * sigmoid_gate).astype(jnp.bfloat16)
        gate_parts = gate_grad.reshape(slots_all, NPE, HID).transpose(1, 0, 2).astype(jnp.float32)
        up_parts = up_grad.reshape(slots_all, NPE, HID).transpose(1, 0, 2).astype(jnp.float32)
        part_grad = jnp.einsum("psh,pdh->psd", gate_parts, gate_w[expert].astype(jnp.float32)) + jnp.einsum("psh,pdh->psd", up_parts, up_w[expert].astype(jnp.float32))
        part_grad = lax.optimization_barrier(part_grad.astype(jnp.bfloat16))
        summed = jnp.sum(part_grad.astype(jnp.float32), axis=0).reshape(N_NODE, MOST, D)
        total = total + jnp.einsum("nqr,nqd->nrd", placing, summed, precision=lax.Precision.HIGHEST)
        return total, None

    start = jnp.zeros((N_NODE, ROWS, D), jnp.float32)
    total, unused = lax.scan(per_expert, start, jnp.arange(EXPERTS, dtype=jnp.int32))
    return total.astype(jnp.bfloat16)
```

```python
import functools

import jax
import jax.numpy as jnp
from jax import lax
from jax.experimental import pallas as pl
from jax.experimental.pallas import tpu as pltpu
from jax.sharding import PartitionSpec as P

MESH = pl.DeviceIdType.MESH
NX, NZ, TEAM, TEAMS, Q = 4, 16, 4, 4, 8
FAR = 11
BF16, F32 = jnp.bfloat16, jnp.float32


def travels(i, s, d):
    if d == 0:
        return s <= 3 - i
    if d == 1:
        return s <= 7 - i
    return jnp.logical_and(s <= 11 - i, i >= 2)


def kernel(
    ny, og_ref, ids_ref, sc_ref, sg_hbm, su_hbm, wg_hbm, wu_hbm, wd_hbm, out_ref,
    sg, su, wg, wu, wd, relay, packed, rbuf, hsend, hrecv, pg, gbuf, fsum, ybuf, ysend, yrecv,
    load_sem, y_send, y_recv, x_send, x_recv, z_send, z_recv, h_send, h_recv,
    b_send, b_recv, c_send, c_recv, o_send, o_recv,
):
    y = lax.axis_index("group")
    node = lax.axis_index("node")
    c = lax.axis_index("tp")
    x, z = node // NZ, lax.rem(node, NZ)
    team, j = z // TEAM, lax.rem(z, TEAM)
    feat = og_ref.shape[1]
    rows = ny * Q

    def at_y(k):
        return {"group": lax.rem(y + k, ny)}

    def at_x(k):
        return {"node": lax.rem(x + k, NX) * NZ + z}

    def at_z(k):
        return {"node": x * NZ + lax.rem(z + k + NZ, NZ)}

    other = {"tp": 1 - c}
    loads = [
        pltpu.make_async_copy(src, dst, load_sem.at[n])
        for n, (src, dst) in enumerate(((sg_hbm, sg), (su_hbm, su), (wd_hbm, wd), (wg_hbm, wg), (wu_hbm, wu)))
    ]
    for load in loads:
        load.start()

    barrier = pltpu.get_barrier_semaphore()
    partners = [at_y(k) for k in range(1, ny)] + [at_x(k) for k in range(1, NX)] + [at_z(1), at_z(-1), other]
    for partner in partners:
        pl.semaphore_signal(barrier, inc=1, device_id=partner, device_id_type=MESH)
    pl.semaphore_wait(barrier, len(partners))

    def remote(src, dst, send, recv, where):
        return pltpu.make_async_remote_copy(
            src_ref=src, dst_ref=dst, send_sem=send, recv_sem=recv, device_id=where, device_id_type=MESH
        )

    def y_copy(k):
        return remote(og_ref, relay.at[y], y_send.at[k], y_recv.at[k], at_y(k))

    for k in range(1, ny):
        y_copy(k).start()
    relay[pl.ds(y, 1)] = og_ref[...][None]

    lanes = NX * TEAMS * Q
    lane = lax.broadcasted_iota(jnp.int32, (rows, lanes), 1)
    expert = lane // Q + y * (NX * TEAMS)
    pick = jnp.zeros((rows, lanes), F32)
    weight = jnp.zeros((rows, lanes), F32)
    ids = ids_ref[...]
    scores = sc_ref[...].astype(F32)
    for k in range(ids.shape[1]):
        hit = ids[:, k : k + 1] == expert
        pick = jnp.where(hit, 1.0, pick)
        weight = jnp.where(hit, scores[:, k : k + 1], weight)
    before = lax.broadcasted_iota(jnp.int32, (rows, rows), 1) < lax.broadcasted_iota(jnp.int32, (rows, rows), 0)
    slot = jnp.dot(before.astype(BF16), pick.astype(BF16), preferred_element_type=F32)
    placed = jnp.logical_and(slot == lax.rem(lane, Q).astype(F32), pick > 0.5)
    place = jnp.where(placed, 1.0, 0.0).astype(BF16)
    place_weight = jnp.where(placed, weight, 0.0).astype(BF16)

    for k in range(1, ny):
        y_copy(k).wait_recv()
    pack = lax.dot_general(
        place, relay[...].reshape(rows, feat), (((0,), (0,)), ((), ())), preferred_element_type=F32
    ).astype(BF16)
    packed[...] = pack.reshape(NX, TEAMS, Q, feat)

    def x_copy(k):
        to = lax.rem(x + k, NX)
        return remote(packed.at[to], rbuf.at[z, :, x], x_send.at[k], x_recv.at[k], at_x(k))

    for k in (2, 1, 3):
        x_copy(k).start()
    rbuf[pl.ds(z, 1), :, pl.ds(x, 1)] = packed[pl.ds(x, 1)][:, :, None]
    for k in range(1, NX):
        x_copy(k).wait_recv()

    def place_of(way, distance):
        src = lax.rem(z - distance + NZ, NZ) if way == 0 else lax.rem(z + distance, NZ)
        at = lax.rem(src, TEAM)
        return src, src // TEAM, (at if way == 0 else TEAM - 1 - at)

    def z_copy(way, s, d):
        src, home, _ = place_of(way, s - 1)
        t = lax.rem(home + (d if way == 0 else TEAMS - d), TEAMS)
        piece = rbuf.at[src, t]
        return remote(piece, piece, z_send.at[way, s, d], z_recv.at[way, s, d], at_z(1 if way == 0 else -1))

    def z_arrive(way, s, d):
        src, home, _ = place_of(way, s)
        t = lax.rem(home + (d if way == 0 else TEAMS - d), TEAMS)
        piece = rbuf.at[src, t]
        return remote(piece, piece, z_send.at[way, s, d], z_recv.at[way, s, d], at_z(1 if way == 0 else -1))

    def z_step(s):
        for d in (2, 1, 0):
            for way in (0, 1):
                if s > 1:
                    _, _, i = place_of(way, s - 1)

                    @pl.when(travels(i, s - 1, d))
                    def _():
                        z_arrive(way, s - 1, d).wait_recv()

                if s <= FAR:
                    _, _, i = place_of(way, s - 1)

                    @pl.when(travels(i, s, d))
                    def _():
                        z_copy(way, s, d).start()

    def hidden_part(n, u):
        rows_in = rbuf[pl.ds(u * TEAM, TEAM), pl.ds(team, 1)].reshape(TEAM * NX * Q, feat)
        hsend[n] = lax.dot_general(rows_in, wd[...], (((1,), (1,)), ((), ())), preferred_element_type=F32)
        h_copy(n).start()

    def h_copy(n):
        return remote(hsend.at[n], hrecv.at[n], h_send.at[n], h_recv.at[n], other)

    def expert_part(n, u):
        h_copy(n).wait_recv()
        grad = hsend[n] + hrecv[n]

        def saved(ref):
            parts = [ref[k, pl.ds(u * TEAM, TEAM)][:, None] for k in range(NX)]
            return jnp.concatenate(parts, axis=1).reshape(TEAM * NX * Q, -1).astype(F32)

        g, up = saved(sg), saved(su)
        s = jax.nn.sigmoid(g)
        gate_grad = (grad * up * s * (1.0 + g * (1.0 - s))).astype(BF16)
        up_grad = (grad * g * s).astype(BF16)
        nt = (((1,), (1,)), ((), ()))
        part = lax.dot_general(gate_grad, wg[...], nt, preferred_element_type=F32)
        part = part + lax.dot_general(up_grad, wu[...], nt, preferred_element_type=F32)
        pg[pl.ds(u * TEAM, TEAM)] = part.astype(BF16).reshape(TEAM, NX, Q, feat)

    for s in range(1, 5):
        z_step(s)
    for load in loads:
        load.wait()
    hidden_part(0, team)
    z_step(5)
    expert_part(0, team)
    for s in range(6, 9):
        z_step(s)
    up_team, down_team = lax.rem(team + 1, TEAMS), lax.rem(team + 3, TEAMS)
    hidden_part(1, up_team)
    hidden_part(2, down_team)
    z_step(9)
    expert_part(1, up_team)
    expert_part(2, down_team)
    for s in range(10, FAR + 2):
        z_step(s)
    across = lax.rem(team + 2, TEAMS)
    hidden_part(3, across)
    expert_part(3, across)

    def b_copy(way, s, d, own_only):
        src, home, _ = place_of(way, s)
        t = lax.rem(home + (d if way == 0 else TEAMS - d), TEAMS)
        piece = gbuf.at[way, src, t]
        return remote(
            pg.at[src] if own_only else piece, piece, b_send.at[way, s, d], b_recv.at[way, s, d],
            at_z(-1 if way == 0 else 1),
        )

    def b_arrive(way, s, d):
        src, home, _ = place_of(way, s)
        t = lax.rem(home + (d if way == 0 else TEAMS - d), TEAMS)
        piece = gbuf.at[way, src, t]
        return remote(
            piece, piece, b_send.at[way, s + 1, d], b_recv.at[way, s + 1, d], at_z(-1 if way == 0 else 1)
        )

    for s in range(FAR, 0, -1):
        for d in (2, 1, 0):
            for way in (0, 1):
                src, home, i = place_of(way, s)
                t = lax.rem(home + (d if way == 0 else TEAMS - d), TEAMS)
                last = travels(i, s, d)
                if s < FAR:
                    further = travels(i, s + 1, d)

                    @pl.when(further)
                    def _():
                        b_arrive(way, s, d).wait_recv()

                        @pl.when(t == team)
                        def _():
                            mine = pg[pl.ds(src, 1)].astype(F32)
                            sofar = gbuf[way, pl.ds(src, 1), pl.ds(t, 1)][0].astype(F32)
                            gbuf[way, pl.ds(src, 1), pl.ds(t, 1)] = (mine + sofar).astype(BF16)[None]

                        b_copy(way, s, d, False).start()

                    last = jnp.logical_and(last, jnp.logical_not(further))

                @pl.when(last)
                def _():
                    b_copy(way, s, d, True).start()

    fsum[...] = jnp.zeros_like(fsum)
    fsum[pl.ds(team, 1)] = pg[pl.ds(z, 1)]
    for d in (0, 1, 2):
        for way in (0, 1):
            _, home, i = place_of(way, 0)
            t = lax.rem(home + (d if way == 0 else TEAMS - d), TEAMS)

            @pl.when(travels(i, 1, d))
            def _():
                b_arrive(way, 0, d).wait_recv()
                came = gbuf[way, pl.ds(z, 1), pl.ds(t, 1)][0].astype(F32)
                fsum[pl.ds(t, 1)] = (fsum[pl.ds(t, 1)].astype(F32) + came).astype(BF16)

    def c_copy(k):
        to = lax.rem(x + k, NX)
        return remote(fsum.at[:, to], ybuf.at[x], c_send.at[k], c_recv.at[k], at_x(k))

    for k in (2, 1, 3):
        c_copy(k).start()
    ybuf[pl.ds(x, 1)] = fsum[:, pl.ds(x, 1)].reshape(1, TEAMS, Q, feat)
    for k in range(1, NX):
        c_copy(k).wait_recv()
    token = jnp.dot(place_weight, ybuf[...].reshape(lanes, feat), preferred_element_type=F32)
    ysend[...] = token.astype(BF16).reshape(ny, Q, feat)

    def o_copy(k):
        return remote(ysend.at[lax.rem(y + k, ny)], yrecv.at[k], o_send.at[k], o_recv.at[k], at_y(k))

    for k in range(1, ny):
        o_copy(k).start()
    total = ysend[pl.ds(y, 1)][0].astype(F32)
    for k in range(1, ny):
        o_copy(k).wait_recv()
        total = total + yrecv[k].astype(F32)
    out_ref[...] = total.astype(BF16)

    for k in range(1, ny):
        y_copy(k).wait_send()
        o_copy(k).wait_send()
    for k in range(1, NX):
        x_copy(k).wait_send()
        c_copy(k).wait_send()
    for n in range(TEAMS):
        h_copy(n).wait_send()
    for s in range(1, FAR + 1):
        for d in (2, 1, 0):
            for way in (0, 1):
                _, _, i = place_of(way, s - 1)

                @pl.when(travels(i, s, d))
                def _():
                    z_copy(way, s, d).wait_send()

                _, _, i = place_of(way, s)

                @pl.when(travels(i, s, d))
                def _():
                    b_copy(way, s, d, False).wait_send()


def per_device(ny, out_grad, expert_ids, gate_scores, saved_gate, saved_up, w_gate, w_up, w_down):
    feat = out_grad.shape[2]
    hid = w_down.shape[1]
    vmem = pl.BlockSpec(memory_space=pltpu.VMEM)
    hbm = pl.BlockSpec(memory_space=pl.ANY)
    saved_shape = (NX, NZ, Q, hid)
    dma = pltpu.SemaphoreType.DMA
    out = pl.pallas_call(
        functools.partial(kernel, ny),
        out_shape=jax.ShapeDtypeStruct((Q, feat), BF16),
        in_specs=[vmem] * 3 + [hbm] * 5,
        out_specs=vmem,
        scratch_shapes=[
            pltpu.VMEM(saved_shape, BF16),
            pltpu.VMEM(saved_shape, BF16),
            pltpu.VMEM((feat, hid), BF16),
            pltpu.VMEM((feat, hid), BF16),
            pltpu.VMEM((hid, feat), BF16),
            pltpu.VMEM((ny, Q, feat), BF16),
            pltpu.VMEM((NX, TEAMS, Q, feat), BF16),
            pltpu.VMEM((NZ, TEAMS, NX, Q, feat), BF16),
            pltpu.VMEM((TEAMS, TEAM * NX * Q, hid), F32),
            pltpu.VMEM((TEAMS, TEAM * NX * Q, hid), F32),
            pltpu.VMEM((NZ, NX, Q, feat), BF16),
            pltpu.VMEM((2, NZ, TEAMS, NX, Q, feat), BF16),
            pltpu.VMEM((TEAMS, NX, Q, feat), BF16),
            pltpu.VMEM((NX, TEAMS, Q, feat), BF16),
            pltpu.VMEM((ny, Q, feat), BF16),
            pltpu.VMEM((ny, Q, feat), BF16),
            dma((5,)),
            dma((ny,)),
            dma((ny,)),
            dma((NX,)),
            dma((NX,)),
            dma((2, FAR + 1, 3)),
            dma((2, FAR + 1, 3)),
            dma((TEAMS,)),
            dma((TEAMS,)),
            dma((2, FAR + 1, 3)),
            dma((2, FAR + 1, 3)),
            dma((NX,)),
            dma((NX,)),
            dma((ny,)),
            dma((ny,)),
        ],
        compiler_params=pltpu.CompilerParams(
            collective_id=0, has_side_effects=True, vmem_limit_bytes=56 * 1024 * 1024
        ),
        name="routed_backward",
    )(
        out_grad[0],
        expert_ids[0],
        gate_scores[0],
        saved_gate.reshape(saved_shape),
        saved_up.reshape(saved_shape),
        w_gate[0],
        w_up[0],
        w_down[0],
    )
    return out[None]


def solution(mesh):
    placed = (
        P("node", "group", "tp"),
        P("node", None, None),
        P("node", None, None),
        P(("group", "node"), None, None, None),
        P(("group", "node"), None, None, None),
        P(("group", "node"), "tp", None),
        P(("group", "node"), "tp", None),
        P(("group", "node"), None, "tp"),
    )
    return jax.shard_map(
        functools.partial(per_device, mesh.shape["group"]),
        mesh=mesh,
        in_specs=placed,
        out_specs=P("node", "group", "tp"),
        check_vma=False,
    )
```

```python
import functools

import jax
import jax.numpy as jnp
from jax import lax
from jax.experimental import pallas as pl
from jax.experimental.pallas import tpu as pltpu
from jax.sharding import PartitionSpec as P

MESH = pl.DeviceIdType.MESH
NX, NZ, TEAM, TEAMS, Q = 4, 16, 4, 4, 8
FAR = 5
RAW = (8, 7)
PAIRS, OWN = 4, 4
META = 128
BF16, F32 = jnp.bfloat16, jnp.float32
NT = (((1,), (1,)), ((), ()))
TN = (((0,), (0,)), ((), ()))


def travels(i, s, d):
    return s <= (3 - i if d == 0 else 5 - i)


def y_steps(p):
    return (4, 3) if p % 2 == 0 else (3, 4)


def kernel(
    ny, og_ref, ids_ref, sc_ref, sg_hbm, su_hbm, wg_hbm, wu_hbm, wd_hbm, out_ref,
    sg, su, wg, wu, wd, msg, raw, yown, ypair, pw_own, pw_pair, packed, xpack, rbuf, zbuf, hsend, hrecv,
    pg, pgz, gbuf, fsum, ybuf, cbuf, tok, tok_own, ysr, yso, rs, zret,
    load_sem, raw_send, raw_recv, y_send, y_recv, xo_send, xo_recv, xz_send, xz_recv, z_send, z_recv,
    h_send, h_recv, b_send, b_recv, co_send, co_recv, cz_send, cz_recv, r_send, r_recv, v_send, v_recv,
):
    y = lax.axis_index("group")
    node = lax.axis_index("node")
    c = lax.axis_index("tp")
    x, z = node // NZ, lax.rem(node, NZ)
    team, j = z // TEAM, lax.rem(z, TEAM)
    feat = og_ref.shape[1]
    rows = ny * Q

    def at_y(k):
        return {"group": lax.rem(y + k + ny, ny)}

    def at_x(k):
        return {"node": lax.rem(x + k, NX) * NZ + z}

    def at_z(k):
        return {"node": x * NZ + lax.rem(z + k + NZ, NZ)}

    other = {"tp": 1 - c}
    loads = [
        pltpu.make_async_copy(src, dst, load_sem.at[n])
        for n, (src, dst) in enumerate(((sg_hbm, sg), (su_hbm, su), (wd_hbm, wd), (wg_hbm, wg), (wu_hbm, wu)))
    ]
    for load in loads:
        load.start()

    barrier = pltpu.get_barrier_semaphore()
    partners = [at_y(1), at_y(-1)] + [at_x(k) for k in range(1, NX)] + [other]
    partners += [at_z(way * k) for k in (1, 3, 4, 5, 6) for way in (1, -1)]
    for partner in partners:
        pl.semaphore_signal(barrier, inc=1, device_id=partner, device_id_type=MESH)

    one = lax.broadcasted_iota(jnp.int32, (rows, rows), 0) == lax.broadcasted_iota(jnp.int32, (rows, rows), 1)
    one = one.astype(BF16)
    ids_t = lax.dot_general(ids_ref[...].astype(F32).astype(BF16), one, TN, preferred_element_type=F32)
    sc_t = lax.dot_general(sc_ref[...], one, TN, preferred_element_type=F32)
    msg[:, :feat] = og_ref[...]
    msg[:, feat:] = jnp.concatenate([ids_t, sc_t], axis=1).astype(BF16)
    yown[pl.ds(y, 1)] = og_ref[...][None]
    pl.semaphore_wait(barrier, len(partners))

    def remote(src, dst, send, recv, where):
        return pltpu.make_async_remote_copy(
            src_ref=src, dst_ref=dst, send_sem=send, recv_sem=recv, device_id=where, device_id_type=MESH
        )

    def raw_first(way):
        k = 6 - j if way == 0 else j + 3
        return remote(
            msg, raw.at[way, k], raw_send.at[way, 0], raw_recv.at[way, k], at_z(k if way == 0 else -k)
        )

    def raw_copy(way, s):
        return remote(
            raw.at[way, s - 1], raw.at[way, s], raw_send.at[way, s], raw_recv.at[way, s], at_z(1 - 2 * way)
        )

    def takes(way, s):
        if s == 3:
            return j == 2 - way, 0
        if s == 4:
            return (j >= 2, 3 - j) if way == 0 else (j <= 1, j)
        if s == 5:
            return (j != 1, (j == 2).astype(jnp.int32) + 1) if way == 0 else (j != 2, 2)
        return True, {(0, 6): 3, (1, 6): 4, (0, 7): 5, (1, 7): 6, (0, 8): 7}[way, s]

    def source(m):
        if m == 0:
            off = jnp.where(j == 0, 4, jnp.where(j == 1, 3, jnp.where(j == 2, -3, -4)))
        elif m == 1:
            off = jnp.where(j == 0, -5, jnp.where(j == 1, 4, jnp.where(j == 2, -4, -5)))
        elif m == 2:
            off = jnp.where(j == 2, -5, 5)
        else:
            off = {3: -6, 4: 6, 5: -7, 6: 7, 7: -8}[m]
        return lax.rem(z + off + NZ, NZ)

    def when(condition):
        if condition is True:
            return lambda body: body()
        return pl.when(condition)

    def raw_step(s):
        for way in (0, 1):
            if s > RAW[way]:
                continue
            condition, m = takes(way, s)

            @when(condition)
            def _():
                raw_copy(way, s).wait_recv()
                if s < RAW[way]:
                    raw_copy(way, s + 1).start()
                block = raw[way, s]
                p, h = m // 2, m % 2
                ypair[pl.ds(p, 1), pl.ds(y, 1), pl.ds(h, 1)] = block[:, :feat][None, None, None]
                place_in(block[:, feat:].astype(F32), m)

    def y_buf(p):
        return yown if p == OWN else ypair.at[p]

    def y_copy(p, way, s):
        piece = y_buf(p).at[lax.rem(y + (1 - s if way == 0 else s - 1) + ny, ny)]
        return remote(piece, piece, y_send.at[p, way, s], y_recv.at[p, way, s], at_y(1 - 2 * way))

    def y_arrive(p, way, s):
        piece = y_buf(p).at[lax.rem(y + (-s if way == 0 else s) + ny, ny)]
        return remote(piece, piece, y_send.at[p, way, s], y_recv.at[p, way, s], at_y(1 - 2 * way))

    def y_step(p, s):
        for way in (0, 1):
            steps = y_steps(p)[way]
            if 2 <= s <= steps + 1:
                y_arrive(p, way, s - 1).wait_recv()
            if s <= steps:
                y_copy(p, way, s).start()

    def placing(meta, expert, place_in_expert):
        shape = expert.shape
        pick = jnp.zeros(shape, F32)
        weight = jnp.zeros(shape, F32)
        for k in range(Q):
            hit = meta[k : k + 1, :rows] == expert
            pick = jnp.where(hit, 1.0, pick)
            weight = jnp.where(hit, meta[k : k + 1, rows:], weight)
        before = lax.broadcasted_iota(jnp.int32, (rows, rows), 0) < lax.broadcasted_iota(jnp.int32, (rows, rows), 1)
        slot = jnp.dot(pick.astype(BF16), before.astype(F32).astype(BF16), preferred_element_type=F32)
        placed = jnp.logical_and(slot == place_in_expert, pick > 0.5)
        return jnp.where(placed, 1.0, 0.0).astype(BF16), jnp.where(placed, weight, 0.0).astype(BF16)

    def place_in(meta, m):
        line = lax.broadcasted_iota(jnp.int32, (NX * Q, rows), 0)
        expert = (line // Q * TEAMS + (y * (NX * TEAMS) + team)).astype(F32)
        place, weighted = placing(meta, expert, lax.rem(line, Q).astype(F32))
        pw_pair[pl.ds(m, 1), pl.ds(0, 1)] = place[None, None]
        pw_pair[pl.ds(m, 1), pl.ds(1, 1)] = weighted[None, None]

    def xz_copy(p, k):
        to = lax.rem(x + k, NX)
        return remote(xpack.at[p, to], zbuf.at[p, x], xz_send.at[p, k], xz_recv.at[p, k], at_x(k))

    def pack_pair(p):
        y_step(p, 5)
        for h in (0, 1):
            packs = jnp.dot(
                pw_pair[2 * p + h, 0], ypair[p, :, h].reshape(rows, feat), preferred_element_type=F32
            ).astype(BF16)
            xpack[p, :, h] = packs.reshape(NX, Q, feat)
        for k in (2, 1, 3):
            xz_copy(p, k).start()
        zbuf[p, pl.ds(x, 1)] = xpack[p, pl.ds(x, 1)]

    def near(d):
        return lax.rem(team + d + TEAMS, TEAMS)

    def xo_copy(d, k):
        to = lax.rem(x + k, NX)
        t = near(d)
        return remote(
            packed.at[t, to], rbuf.at[z, t, x], xo_send.at[d + 1, k], xo_recv.at[d + 1, k], at_x(k)
        )

    def pack_own():
        y_step(OWN, 5)
        line = lax.broadcasted_iota(jnp.int32, (TEAMS * NX * Q, rows), 0)
        expert = lax.rem(line // Q, NX) * TEAMS + line // (NX * Q) + y * (NX * TEAMS)
        place, weighted = placing(msg[:, feat:].astype(F32), expert.astype(F32), lax.rem(line, Q).astype(F32))
        pw_own[...] = weighted
        packs = jnp.dot(place, yown[...].reshape(rows, feat), preferred_element_type=F32).astype(BF16)
        packed[...] = packs.reshape(TEAMS, NX, Q, feat)
        for d in (1, -1, 0):
            for k in (2, 1, 3):
                xo_copy(d, k).start()
        rbuf[pl.ds(z, 1), :, pl.ds(x, 1)] = packed[:, pl.ds(x, 1)][None]

    def place_of(way, distance):
        src = lax.rem(z - distance + NZ, NZ) if way == 0 else lax.rem(z + distance, NZ)
        at = lax.rem(src, TEAM)
        return src, src // TEAM, (at if way == 0 else TEAM - 1 - at)

    def piece_of(way, distance, d):
        src, home, _ = place_of(way, distance)
        return src, lax.rem(home + (d if way == 0 else TEAMS - d), TEAMS)

    def z_copy(way, s, d, distance):
        src, t = piece_of(way, distance, d)
        piece = rbuf.at[src, t]
        return remote(piece, piece, z_send.at[way, s, d], z_recv.at[way, s, d], at_z(1 - 2 * way))

    def z_step(s):
        for d in (1, 0):
            for way in (0, 1):
                _, _, i = place_of(way, s - 1)
                if s > 1:

                    @pl.when(travels(i, s - 1, d))
                    def _():
                        z_copy(way, s - 1, d, s - 1).wait_recv()

                if s <= FAR:

                    @pl.when(travels(i, s, d))
                    def _():
                        z_copy(way, s, d, s - 1).start()

    def h_copy(n):
        return remote(hsend.at[n], hrecv.at[n], h_send.at[n], h_recv.at[n], other)

    def hidden_part(n, rows_in):
        hsend[n] = lax.dot_general(rows_in.reshape(-1, feat), wd[...], NT, preferred_element_type=F32)
        h_copy(n).start()

    def expert_part(n, saved):
        h_copy(n).wait_recv()
        grad = hsend[n] + hrecv[n]
        g, up = saved(sg), saved(su)
        s = jax.nn.sigmoid(g)
        gate_grad = (grad * up * s * (1.0 + g * (1.0 - s))).astype(BF16)
        up_grad = (grad * g * s).astype(BF16)
        part = lax.dot_general(gate_grad, wg[...], NT, preferred_element_type=F32)
        part = part + lax.dot_general(up_grad, wu[...], NT, preferred_element_type=F32)
        return part.astype(BF16)

    def team_hidden(n, u):
        hidden_part(n, rbuf[pl.ds(u * TEAM, TEAM), pl.ds(team, 1)])

    def team_expert(n, u):
        def saved(ref):
            parts = [ref[k, pl.ds(u * TEAM, TEAM)][:, None] for k in range(NX)]
            return jnp.concatenate(parts, axis=1).reshape(TEAM * NX * Q, -1).astype(F32)

        pg[pl.ds(u * TEAM, TEAM)] = expert_part(n, saved).reshape(TEAM, NX, Q, feat)

    def pairs_hidden(n, first):
        for p in (first, first + 1):
            for k in range(1, NX):
                xz_copy(p, k).wait_recv()
        hidden_part(n, zbuf[pl.ds(first, 2)])

    def pairs_expert(n, first):
        def saved(ref):
            parts = [
                ref[k, pl.ds(source(2 * p + h), 1)]
                for p in (first, first + 1)
                for k in range(NX)
                for h in (0, 1)
            ]
            return jnp.concatenate(parts, axis=0).reshape(2 * NX * 2 * Q, -1).astype(F32)

        pgz[pl.ds(first, 2)] = expert_part(n, saved).reshape(2, NX, 2, Q, feat)
        for p in (first + 1, first):
            for k in (2, 1, 3):
                cz_copy(p, k).start()
            cbuf[p, pl.ds(x, 1)] = pgz[p, pl.ds(x, 1)]

    def b_copy(way, s, d, own_only):
        src, t = piece_of(way, s, d)
        piece = gbuf.at[way, src, t]
        return remote(
            pg.at[src] if own_only else piece, piece, b_send.at[way, s, d], b_recv.at[way, s, d],
            at_z(2 * way - 1),
        )

    def b_arrive(way, s, d):
        src, t = piece_of(way, s, d)
        piece = gbuf.at[way, src, t]
        return remote(piece, piece, b_send.at[way, s + 1, d], b_recv.at[way, s + 1, d], at_z(2 * way - 1))

    def b_step(s):
        for d in (1, 0):
            for way in (0, 1):
                _, _, i = place_of(way, s)
                src, t = piece_of(way, s, d)
                last = travels(i, s, d)
                if s < FAR:
                    further = travels(i, s + 1, d)

                    @pl.when(further)
                    def _():
                        b_arrive(way, s, d).wait_recv()

                        @pl.when(t == team)
                        def _():
                            mine = pg[pl.ds(src, 1)].astype(F32)
                            sofar = gbuf[way, pl.ds(src, 1), pl.ds(t, 1)][0].astype(F32)
                            gbuf[way, pl.ds(src, 1), pl.ds(t, 1)] = (mine + sofar).astype(BF16)[None]

                        b_copy(way, s, d, False).start()

                    last = jnp.logical_and(last, jnp.logical_not(further))

                @pl.when(last)
                def _():
                    b_copy(way, s, d, True).start()

    def came(way, d):
        b_arrive(way, 0, d).wait_recv()
        _, t = piece_of(way, 0, d)
        return gbuf[way, pl.ds(z, 1), pl.ds(t, 1)][0]

    def co_copy(d, k):
        to = lax.rem(x + k, NX)
        t = near(d)
        return remote(fsum.at[t, to], ybuf.at[t, x], co_send.at[d + 1, k], co_recv.at[d + 1, k], at_x(k))

    def cz_copy(p, k):
        to = lax.rem(x + k, NX)
        return remote(pgz.at[p, to], cbuf.at[p, x], cz_send.at[p, k], cz_recv.at[p, k], at_x(k))

    def to_relay(d):
        for k in (2, 1, 3):
            co_copy(d, k).start()
        t = near(d)
        ybuf[pl.ds(t, 1), pl.ds(x, 1)] = fsum[pl.ds(t, 1), pl.ds(x, 1)]

    def finish_tree():
        for way, d in ((0, 1), (1, -1)):
            fsum[pl.ds(near(d), 1)] = came(way, 1)
            to_relay(d)
        fsum[pl.ds(team, 1)] = pg[pl.ds(z, 1)]
        for way in (0, 1):
            _, _, i = place_of(way, 0)

            @pl.when(travels(i, 1, 0))
            def _():
                got = came(way, 0).astype(F32)
                fsum[pl.ds(team, 1)] = (fsum[pl.ds(team, 1)].astype(F32) + got).astype(BF16)

        to_relay(0)

    def combine_pair(p):
        for k in range(1, NX):
            cz_copy(p, k).wait_recv()
        for h in (0, 1):
            token = lax.dot_general(
                pw_pair[2 * p + h, 1], cbuf[p, :, h].reshape(NX * Q, feat), TN, preferred_element_type=F32
            )
            tok[p, :, h] = token.astype(BF16).reshape(ny, Q, feat)

    def combine_own():
        ybuf[pl.ds(near(2), 1)] = jnp.zeros((1, NX, Q, feat), BF16)
        for d in (1, -1, 0):
            for k in range(1, NX):
                co_copy(d, k).wait_recv()
        token = lax.dot_general(pw_own[...], ybuf[...].reshape(-1, feat), TN, preferred_element_type=F32)
        tok_own[...] = token.astype(BF16).reshape(ny, Q, feat)

    def r_bufs(p):
        return (tok_own, yso) if p == OWN else (tok.at[p], ysr.at[p])

    def r_target(p, way, s):
        left = y_steps(p)[way] + 1 - s
        return lax.rem(y + (left if way == 0 else -left) + ny, ny)

    def r_copy(p, way, s):
        mine, sums = r_bufs(p)
        src = mine.at[r_target(p, way, s)] if s == 1 else sums.at[way, s - 1]
        return remote(src, sums.at[way, s], r_send.at[p, way, s], r_recv.at[p, way, s], at_y(1 - 2 * way))

    def r_step(p, s):
        mine, sums = r_bufs(p)
        for way in (0, 1):
            steps = y_steps(p)[way]
            if 2 <= s <= steps + 1:
                r_copy(p, way, s - 1).wait_recv()
            if s <= steps:
                if s > 1:
                    term = mine[pl.ds(r_target(p, way, s), 1)][0].astype(F32)
                    sums[way, s - 1] = (sums[way, s - 1].astype(F32) + term).astype(BF16)
                r_copy(p, way, s).start()

    def r_total(p):
        r_step(p, 5)
        mine, sums = r_bufs(p)
        total = mine[pl.ds(y, 1)][0].astype(F32)
        for way in (0, 1):
            total = total + sums[way, y_steps(p)[way]].astype(F32)
        return total

    def r_finish(p):
        rs[pl.ds(2 * p, 2)] = r_total(p)

    def v_copy(way, s, first):
        to, where = (0, s) if first else (s - 1, 1)
        return remote(
            zret.at[way, s], zret.at[way, to], v_send.at[way, s], v_recv.at[way, to],
            at_z(-where if way == 0 else where),
        )

    def v_cases(way, s):
        condition, _ = takes(way, s)
        if s > 6:
            return ((True, False),)
        end = j == 2 - way
        if s == 3:
            return ((condition, True),)
        rest = jnp.logical_not(end)
        if condition is True:
            return ((end, True), (rest, False))
        return ((jnp.logical_and(condition, end), True), (jnp.logical_and(condition, rest), False))

    def v_step(s, way):
        condition, m = takes(way, s)

        @when(condition)
        def _():
            total = rs[pl.ds(m, 1)][0]
            if s < RAW[way]:
                v_copy(way, s + 1, False).wait_recv()
                total = total + zret[way, s].astype(F32)
            zret[way, s] = total.astype(BF16)

        for condition, first in v_cases(way, s):

            @when(condition)
            def _():
                v_copy(way, s, first).start()

    y_step(OWN, 1)
    raw_first(0).start()
    raw_first(1).start()
    raw_step(3)
    y_step(OWN, 2)
    raw_step(4)
    y_step(OWN, 3)
    raw_step(5)
    y_step(0, 1)
    y_step(OWN, 4)
    raw_step(6)
    y_step(1, 1)
    y_step(0, 2)
    pack_own()
    raw_step(7)
    y_step(2, 1)
    y_step(1, 2)
    y_step(0, 3)
    for d in (1, -1, 0):
        for k in range(1, NX):
            xo_copy(d, k).wait_recv()
    z_step(1)
    raw_step(8)
    y_step(3, 1)
    y_step(2, 2)
    y_step(1, 3)
    y_step(0, 4)
    z_step(2)
    y_step(3, 2)
    y_step(2, 3)
    y_step(1, 4)
    pack_pair(0)
    z_step(3)
    y_step(3, 3)
    y_step(2, 4)
    pack_pair(1)
    z_step(4)
    y_step(3, 4)
    pack_pair(2)
    for load in loads:
        load.wait()
    team_hidden(0, team)
    z_step(5)
    pack_pair(3)
    team_expert(0, team)
    z_step(6)
    beside = lax.rem(team + 3 - 2 * (j // 2), TEAMS)
    team_hidden(1, beside)
    pairs_hidden(2, 0)
    team_expert(1, beside)
    b_step(5)
    pairs_hidden(3, 2)
    pairs_expert(2, 0)
    b_step(4)
    pairs_expert(3, 2)
    b_step(3)
    combine_pair(3)
    r_step(3, 1)
    combine_pair(2)
    r_step(2, 1)
    r_step(3, 2)
    b_step(2)
    combine_pair(1)
    r_step(1, 1)
    r_step(2, 2)
    r_step(3, 3)
    combine_pair(0)
    r_step(0, 1)
    r_step(1, 2)
    r_step(2, 3)
    r_step(3, 4)
    b_step(1)
    r_finish(3)
    v_step(8, 0)
    v_step(7, 1)
    r_step(0, 2)
    r_step(1, 3)
    r_step(2, 4)
    finish_tree()
    r_finish(2)
    v_step(7, 0)
    v_step(6, 1)
    r_step(0, 3)
    r_step(1, 4)
    combine_own()
    r_step(OWN, 1)
    r_finish(1)
    v_step(6, 0)
    r_step(0, 4)
    r_step(OWN, 2)
    r_finish(0)
    for s in (5, 4, 3):
        for way in (0, 1):
            v_step(s, way)
        if s > 3:
            r_step(OWN, 8 - s)
    total = r_total(OWN)
    for way in (0, 1):
        v_copy(way, 1, False).wait_recv()
        total = total + zret[way, 0].astype(F32)
    out_ref[...] = total.astype(BF16)

    for way in (0, 1):
        raw_first(way).wait_send()
        for s in range(3, RAW[way] + 1):
            condition, _ = takes(way, s)
            if s < RAW[way]:

                @when(condition)
                def _():
                    raw_copy(way, s + 1).wait_send()

            @when(condition)
            def _():
                v_copy(way, s, False).wait_send()

        for p in range(PAIRS + 1):
            for s in range(1, y_steps(p)[way] + 1):
                y_copy(p, way, s).wait_send()
                r_copy(p, way, s).wait_send()
    for k in range(1, NX):
        for d in (1, -1, 0):
            xo_copy(d, k).wait_send()
            co_copy(d, k).wait_send()
        for p in range(PAIRS):
            xz_copy(p, k).wait_send()
            cz_copy(p, k).wait_send()
    for n in range(TEAMS):
        h_copy(n).wait_send()
    for s in range(1, FAR + 1):
        for d in (1, 0):
            for way in (0, 1):
                _, _, i = place_of(way, s - 1)

                @pl.when(travels(i, s, d))
                def _():
                    z_copy(way, s, d, s - 1).wait_send()

                _, _, i = place_of(way, s)

                @pl.when(travels(i, s, d))
                def _():
                    b_copy(way, s, d, False).wait_send()


def per_device(ny, out_grad, expert_ids, gate_scores, saved_gate, saved_up, w_gate, w_up, w_down):
    feat = out_grad.shape[2]
    hid = w_down.shape[1]
    vmem = pl.BlockSpec(memory_space=pltpu.VMEM)
    hbm = pl.BlockSpec(memory_space=pl.ANY)
    saved_shape = (NX, NZ, Q, hid)
    rows = ny * Q
    chunk = TEAM * NX * Q

    def sems(*shape):
        return [pltpu.SemaphoreType.DMA(shape)] * 2

    out = pl.pallas_call(
        functools.partial(kernel, ny),
        out_shape=jax.ShapeDtypeStruct((Q, feat), BF16),
        in_specs=[vmem] * 3 + [hbm] * 5,
        out_specs=vmem,
        scratch_shapes=[
            pltpu.VMEM(saved_shape, BF16),
            pltpu.VMEM(saved_shape, BF16),
            pltpu.VMEM((feat, hid), BF16),
            pltpu.VMEM((feat, hid), BF16),
            pltpu.VMEM((hid, feat), BF16),
            pltpu.VMEM((Q, feat + META), BF16),
            pltpu.VMEM((2, RAW[0] + 1, Q, feat + META), BF16),
            pltpu.VMEM((ny, Q, feat), BF16),
            pltpu.VMEM((PAIRS, ny, 2, Q, feat), BF16),
            pltpu.VMEM((TEAMS * NX * Q, rows), BF16),
            pltpu.VMEM((2 * PAIRS, 2, NX * Q, rows), BF16),
            pltpu.VMEM((TEAMS, NX, Q, feat), BF16),
            pltpu.VMEM((PAIRS, NX, 2, Q, feat), BF16),
            pltpu.VMEM((NZ, TEAMS, NX, Q, feat), BF16),
            pltpu.VMEM((PAIRS, NX, 2, Q, feat), BF16),
            pltpu.VMEM((4, chunk, hid), F32),
            pltpu.VMEM((4, chunk, hid), F32),
            pltpu.VMEM((NZ, NX, Q, feat), BF16),
            pltpu.VMEM((PAIRS, NX, 2, Q, feat), BF16),
            pltpu.VMEM((2, NZ, TEAMS, NX, Q, feat), BF16),
            pltpu.VMEM((TEAMS, NX, Q, feat), BF16),
            pltpu.VMEM((TEAMS, NX, Q, feat), BF16),
            pltpu.VMEM((PAIRS, NX, 2, Q, feat), BF16),
            pltpu.VMEM((PAIRS, ny, 2, Q, feat), BF16),
            pltpu.VMEM((ny, Q, feat), BF16),
            pltpu.VMEM((PAIRS, 2, 5, 2, Q, feat), BF16),
            pltpu.VMEM((2, 5, Q, feat), BF16),
            pltpu.VMEM((2 * PAIRS, Q, feat), F32),
            pltpu.VMEM((2, RAW[0] + 1, Q, feat), BF16),
            pltpu.SemaphoreType.DMA((5,)),
            *sems(2, RAW[0] + 1),
            *sems(PAIRS + 1, 2, 5),
            *sems(3, NX),
            *sems(PAIRS, NX),
            *sems(2, FAR + 1, 2),
            *sems(4),
            *sems(2, FAR + 1, 2),
            *sems(3, NX),
            *sems(PAIRS, NX),
            *sems(PAIRS + 1, 2, 5),
            *sems(2, RAW[0] + 1),
        ],
        compiler_params=pltpu.CompilerParams(
            collective_id=0, has_side_effects=True, vmem_limit_bytes=56 * 1024 * 1024
        ),
        name="routed_backward",
    )(
        out_grad[0],
        expert_ids[0],
        gate_scores[0],
        saved_gate.reshape(saved_shape),
        saved_up.reshape(saved_shape),
        w_gate[0],
        w_up[0],
        w_down[0],
    )
    return out[None]


def solution(mesh):
    placed = (
        P("node", "group", "tp"),
        P("node", None, None),
        P("node", None, None),
        P(("group", "node"), None, None, None),
        P(("group", "node"), None, None, None),
        P(("group", "node"), "tp", None),
        P(("group", "node"), "tp", None),
        P(("group", "node"), None, "tp"),
    )
    return jax.shard_map(
        functools.partial(per_device, mesh.shape["group"]),
        mesh=mesh,
        in_specs=placed,
        out_specs=P("node", "group", "tp"),
        check_vma=False,
    )
```

```python
import functools

import jax
import jax.numpy as jnp
from jax import lax
from jax.experimental import pallas as pl
from jax.experimental.pallas import tpu as pltpu
from jax.sharding import PartitionSpec as P

MESH = pl.DeviceIdType.MESH
NX, NZ, TEAM, TEAMS, Q = 4, 16, 4, 4, 8
FAR = 5
PAIRS = 4
META = 128
BF16, F32 = jnp.bfloat16, jnp.float32
NT = (((1,), (1,)), ((), ()))
TN = (((0,), (0,)), ((), ()))


def travels(i, s, d):
    return s <= (3 - i if d == 0 else 5 - i)


def y_steps(p):
    return (4, 3) if p % 2 == 0 else (3, 4)


def kernel(
    ny, og_ref, ids_ref, sc_ref, sg_hbm, su_hbm, wg_hbm, wu_hbm, wd_hbm, out_ref,
    sg, su, wg, wu, wd, msg, raw, yown, ypair, pw_own, pw_pair, packed, xpack, rbuf, zbuf, hsend, hrecv,
    pg, pgz, gbuf, fsum, ybuf, cbuf, tok, tok_own, ysr, ylast, rs, vmid, vfin,
    load_sem, raw_send, raw_recv, own_send, own_recv, y_send, y_recv, xo_send, xo_recv, xz_send, xz_recv, z_send, z_recv,
    h_send, h_recv, b_send, b_recv, co_send, co_recv, cz_send, cz_recv, r_send, r_recv, last_send, last_recv,
    v_send, v_recv, f_send, f_recv,
):
    y = lax.axis_index("group")
    node = lax.axis_index("node")
    c = lax.axis_index("tp")
    x, z = node // NZ, lax.rem(node, NZ)
    team, j = z // TEAM, lax.rem(z, TEAM)
    feat = og_ref.shape[1]
    rows = ny * Q

    def at_y(k):
        return {"group": lax.rem(y + k + ny, ny)}

    def at_x(k):
        return {"node": lax.rem(x + k, NX) * NZ + z}

    def at_z(k):
        return {"node": x * NZ + lax.rem(z + k + NZ, NZ)}

    other = {"tp": 1 - c}
    loads = [
        pltpu.make_async_copy(src, dst, load_sem.at[n])
        for n, (src, dst) in enumerate(((sg_hbm, sg), (su_hbm, su), (wd_hbm, wd), (wg_hbm, wg), (wu_hbm, wu)))
    ]
    for load in loads:
        load.start()

    barrier = pltpu.get_barrier_semaphore()
    base = (5 + j - 4 * (j // 2), 8 - j - 4 * ((3 - j) // 2))
    relays = (j + 1) % 2
    partners = [at_y(k) for k in range(1, ny)] + [at_x(k) for k in range(1, NX)] + [other, at_z(1), at_z(-1)]
    partners += [at_z(6 - j), at_z(8 - j), at_z(-3 - j), at_z(-5 - j)]
    partners += [at_z(jnp.where(relays == 1, -base[0] - n, base[1] + n)) for n in range(PAIRS)]
    for partner in partners:
        pl.semaphore_signal(barrier, inc=1, device_id=partner, device_id_type=MESH)

    msg[:, :feat] = og_ref[...]
    msg[:, feat:] = jnp.concatenate([ids_ref[...].astype(F32), sc_ref[...].astype(F32)], axis=1).astype(BF16)
    yown[pl.ds(y, 1)] = og_ref[...][None]
    pl.semaphore_wait(barrier, len(partners))

    def remote(src, dst, send, recv, where):
        return pltpu.make_async_remote_copy(
            src_ref=src, dst_ref=dst, send_sem=send, recv_sem=recv, device_id=where, device_id_type=MESH
        )

    def raw_first(way, far):
        k = (8 if far else 6) - j if way == 0 else (5 if far else 3) + j
        n = 3 - j if way == 0 else j
        return remote(
            msg, raw.at[way, n], raw_send.at[way, far], raw_recv.at[way, n], at_z(k if way == 0 else -k)
        )

    def raw_copy(way, n):
        piece = raw.at[way, n]
        return remote(piece, piece, raw_send.at[way, 2 + n], raw_recv.at[way, n], at_z(1 - 2 * way))

    def hands_on(way):
        return relays == 1 - way

    def source(way, n):
        return lax.rem(z + (-base[0] - n if way == 0 else base[1] + n) + NZ, NZ)

    def raw_relay(n):
        for way in (0, 1):

            @pl.when(hands_on(way))
            def _():
                raw_copy(way, n).wait_recv()
                raw_copy(way, n).start()

    def raw_take(n):
        for way in (0, 1):

            @pl.when(jnp.logical_not(hands_on(way)))
            def _():
                raw_copy(way, n).wait_recv()

            block = raw[way, n]
            ypair[n, pl.ds(y, 1), way] = block[:, :feat][None]
            place_in(block[:, feat:].astype(F32), n, way)

    def own_copy(k):
        return remote(og_ref, yown.at[y], own_send.at[k], own_recv.at[k], at_y(k))

    def y_copy(p, way, s):
        piece = ypair.at[p, lax.rem(y + (1 - s if way == 0 else s - 1) + ny, ny)]
        return remote(piece, piece, y_send.at[p, way, s], y_recv.at[p, way, s], at_y(1 - 2 * way))

    def y_arrive(p, way, s):
        piece = ypair.at[p, lax.rem(y + (-s if way == 0 else s) + ny, ny)]
        return remote(piece, piece, y_send.at[p, way, s], y_recv.at[p, way, s], at_y(1 - 2 * way))

    def y_step(p, s):
        for way in (0, 1):
            steps = y_steps(p)[way]
            if 2 <= s <= steps + 1:
                y_arrive(p, way, s - 1).wait_recv()
            if s <= steps:
                y_copy(p, way, s).start()

    def placing(meta, expert, place_in_expert):
        shape = expert.shape
        pick = jnp.zeros(shape, F32)
        weight = jnp.zeros(shape, F32)
        for k in range(Q):
            hit = meta[k : k + 1, :rows] == expert
            pick = jnp.where(hit, 1.0, pick)
            weight = jnp.where(hit, meta[k : k + 1, rows:], weight)
        before = lax.broadcasted_iota(jnp.int32, (rows, rows), 0) < lax.broadcasted_iota(jnp.int32, (rows, rows), 1)
        slot = jnp.dot(pick.astype(BF16), before.astype(F32).astype(BF16), preferred_element_type=F32)
        placed = jnp.logical_and(slot == place_in_expert, pick > 0.5)
        return jnp.where(placed, 1.0, 0.0).astype(BF16), jnp.where(placed, weight, 0.0).astype(BF16)

    def place_in(meta, p, way):
        line = lax.broadcasted_iota(jnp.int32, (NX * Q, rows), 0)
        expert = (line // Q * TEAMS + (y * (NX * TEAMS) + team)).astype(F32)
        place, weighted = placing(meta, expert, lax.rem(line, Q).astype(F32))
        pw_pair[p, way, 0] = place
        pw_pair[p, way, 1] = weighted

    def xz_copy(p, k):
        to = lax.rem(x + k, NX)
        return remote(xpack.at[p, to], zbuf.at[p, x], xz_send.at[p, k], xz_recv.at[p, k], at_x(k))

    def pack_pair(p):
        y_step(p, 5)
        for h in (0, 1):
            packs = jnp.dot(
                pw_pair[p, h, 0], ypair[p, :, h].reshape(rows, feat), preferred_element_type=F32
            ).astype(BF16)
            xpack[p, :, h] = packs.reshape(NX, Q, feat)
        for k in (2, 1, 3):
            xz_copy(p, k).start()
        zbuf[p, pl.ds(x, 1)] = xpack[p, pl.ds(x, 1)]

    def near(d):
        return lax.rem(team + d + TEAMS, TEAMS)

    def xo_copy(d, k):
        to = lax.rem(x + k, NX)
        t = near(d)
        return remote(
            packed.at[t, to], rbuf.at[z, t, x], xo_send.at[d + 1, k], xo_recv.at[d + 1, k], at_x(k)
        )

    def place_own():
        line = lax.broadcasted_iota(jnp.int32, (TEAMS * NX * Q, rows), 0)
        expert = lax.rem(line // Q, NX) * TEAMS + line // (NX * Q) + y * (NX * TEAMS)
        place, weighted = placing(msg[:, feat:].astype(F32), expert.astype(F32), lax.rem(line, Q).astype(F32))
        pw_own[0] = place
        pw_own[1] = weighted

    def pack_own():
        for k in range(1, ny):
            own_copy(k).wait_recv()
        packs = jnp.dot(pw_own[0], yown[...].reshape(rows, feat), preferred_element_type=F32).astype(BF16)
        packed[...] = packs.reshape(TEAMS, NX, Q, feat)
        for d in (1, -1, 0):
            for k in (2, 1, 3):
                xo_copy(d, k).start()
        rbuf[pl.ds(z, 1), :, pl.ds(x, 1)] = packed[:, pl.ds(x, 1)][None]

    def place_of(way, distance):
        src = lax.rem(z - distance + NZ, NZ) if way == 0 else lax.rem(z + distance, NZ)
        at = lax.rem(src, TEAM)
        return src, src // TEAM, (at if way == 0 else TEAM - 1 - at)

    def piece_of(way, distance, d):
        src, home, _ = place_of(way, distance)
        return src, lax.rem(home + (d if way == 0 else TEAMS - d), TEAMS)

    def z_copy(way, s, d, distance):
        src, t = piece_of(way, distance, d)
        piece = rbuf.at[src, t]
        return remote(piece, piece, z_send.at[way, s, d], z_recv.at[way, s, d], at_z(1 - 2 * way))

    def z_step(s):
        for d in (1, 0):
            for way in (0, 1):
                _, _, i = place_of(way, s - 1)
                if s > 1:

                    @pl.when(travels(i, s - 1, d))
                    def _():
                        z_copy(way, s - 1, d, s - 1).wait_recv()

                if s <= FAR:

                    @pl.when(travels(i, s, d))
                    def _():
                        z_copy(way, s, d, s - 1).start()

    def h_copy(n):
        return remote(hsend.at[n], hrecv.at[n], h_send.at[n], h_recv.at[n], other)

    def hidden_part(n, rows_in):
        hsend[n] = lax.dot_general(rows_in.reshape(-1, feat), wd[...], NT, preferred_element_type=F32)
        h_copy(n).start()

    def expert_part(n, saved):
        h_copy(n).wait_recv()
        grad = hsend[n] + hrecv[n]
        g, up = saved(sg), saved(su)
        s = jax.nn.sigmoid(g)
        gate_grad = (grad * up * s * (1.0 + g * (1.0 - s))).astype(BF16)
        up_grad = (grad * g * s).astype(BF16)
        part = lax.dot_general(gate_grad, wg[...], NT, preferred_element_type=F32)
        part = part + lax.dot_general(up_grad, wu[...], NT, preferred_element_type=F32)
        return part.astype(BF16)

    def team_hidden(n, u):
        hidden_part(n, rbuf[pl.ds(u * TEAM, TEAM), pl.ds(team, 1)])

    def team_expert(n, u):
        def saved(ref):
            parts = [ref[k, pl.ds(u * TEAM, TEAM)][:, None] for k in range(NX)]
            return jnp.concatenate(parts, axis=1).reshape(TEAM * NX * Q, -1).astype(F32)

        pg[pl.ds(u * TEAM, TEAM)] = expert_part(n, saved).reshape(TEAM, NX, Q, feat)

    def pairs_hidden(n, first):
        for p in (first, first + 1):
            for k in range(1, NX):
                xz_copy(p, k).wait_recv()
        hidden_part(n, zbuf[pl.ds(first, 2)])

    def pairs_expert(n, first):
        def saved(ref):
            parts = [
                ref[k, pl.ds(source(h, p), 1)]
                for p in (first, first + 1)
                for k in range(NX)
                for h in (0, 1)
            ]
            return jnp.concatenate(parts, axis=0).reshape(2 * NX * 2 * Q, -1).astype(F32)

        pgz[pl.ds(first, 2)] = expert_part(n, saved).reshape(2, NX, 2, Q, feat)
        for p in (first, first + 1):
            for k in (2, 1, 3):
                cz_copy(p, k).start()
            cbuf[p, pl.ds(x, 1)] = pgz[p, pl.ds(x, 1)]

    def b_copy(way, s, d, own_only):
        src, t = piece_of(way, s, d)
        piece = gbuf.at[way, src, t]
        return remote(
            pg.at[src] if own_only else piece, piece, b_send.at[way, s, d], b_recv.at[way, s, d],
            at_z(2 * way - 1),
        )

    def b_arrive(way, s, d):
        src, t = piece_of(way, s, d)
        piece = gbuf.at[way, src, t]
        return remote(piece, piece, b_send.at[way, s + 1, d], b_recv.at[way, s + 1, d], at_z(2 * way - 1))

    def b_step(s):
        for d in (1, 0):
            for way in (0, 1):
                _, _, i = place_of(way, s)
                src, t = piece_of(way, s, d)
                last = travels(i, s, d)
                if s < FAR:
                    further = travels(i, s + 1, d)

                    @pl.when(further)
                    def _():
                        b_arrive(way, s, d).wait_recv()

                        @pl.when(t == team)
                        def _():
                            mine = pg[pl.ds(src, 1)].astype(F32)
                            sofar = gbuf[way, pl.ds(src, 1), pl.ds(t, 1)][0].astype(F32)
                            gbuf[way, pl.ds(src, 1), pl.ds(t, 1)] = (mine + sofar).astype(BF16)[None]

                        b_copy(way, s, d, False).start()

                    last = jnp.logical_and(last, jnp.logical_not(further))

                @pl.when(last)
                def _():
                    b_copy(way, s, d, True).start()

    def came(way, d):
        b_arrive(way, 0, d).wait_recv()
        _, t = piece_of(way, 0, d)
        return gbuf[way, pl.ds(z, 1), pl.ds(t, 1)][0]

    def co_copy(d, k):
        to = lax.rem(x + k, NX)
        t = near(d)
        return remote(fsum.at[t, to], ybuf.at[t, x], co_send.at[d + 1, k], co_recv.at[d + 1, k], at_x(k))

    def cz_copy(p, k):
        to = lax.rem(x + k, NX)
        return remote(pgz.at[p, to], cbuf.at[p, x], cz_send.at[p, k], cz_recv.at[p, k], at_x(k))

    def to_relay(d):
        for k in (2, 1, 3):
            co_copy(d, k).start()
        t = near(d)
        ybuf[pl.ds(t, 1), pl.ds(x, 1)] = fsum[pl.ds(t, 1), pl.ds(x, 1)]

    def finish_tree():
        for way, d in ((0, 1), (1, -1)):
            fsum[pl.ds(near(d), 1)] = came(way, 1)
            to_relay(d)
        fsum[pl.ds(team, 1)] = pg[pl.ds(z, 1)]
        for way in (0, 1):
            _, _, i = place_of(way, 0)

            @pl.when(travels(i, 1, 0))
            def _():
                got = came(way, 0).astype(F32)
                fsum[pl.ds(team, 1)] = (fsum[pl.ds(team, 1)].astype(F32) + got).astype(BF16)

        to_relay(0)

    def combine_pair(p):
        for k in range(1, NX):
            cz_copy(p, k).wait_recv()
        for h in (0, 1):
            token = lax.dot_general(
                pw_pair[p, h, 1], cbuf[p, :, h].reshape(NX * Q, feat), TN, preferred_element_type=F32
            )
            tok[p, :, h] = token.astype(BF16).reshape(ny, Q, feat)

    def combine_own():
        ybuf[pl.ds(near(2), 1)] = jnp.zeros((1, NX, Q, feat), BF16)
        for d in (1, -1, 0):
            for k in range(1, NX):
                co_copy(d, k).wait_recv()
        token = lax.dot_general(pw_own[1], ybuf[...].reshape(-1, feat), TN, preferred_element_type=F32)
        tok_own[...] = token.astype(BF16).reshape(ny, Q, feat)

    def last_copy(k):
        return remote(
            tok_own.at[lax.rem(y + k, ny)], ylast.at[k], last_send.at[k], last_recv.at[k], at_y(k)
        )

    def r_target(p, way, s):
        left = y_steps(p)[way] + 1 - s
        return lax.rem(y + (left if way == 0 else -left) + ny, ny)

    def r_copy(p, way, s):
        src = tok.at[p, r_target(p, way, s)] if s == 1 else ysr.at[p, way, s - 1]
        return remote(src, ysr.at[p, way, s], r_send.at[p, way, s], r_recv.at[p, way, s], at_y(1 - 2 * way))

    def r_step(p, s):
        for way in (0, 1):
            steps = y_steps(p)[way]
            if 2 <= s <= steps + 1:
                r_copy(p, way, s - 1).wait_recv()
            if s <= steps:
                if s > 1:
                    term = tok[p, pl.ds(r_target(p, way, s), 1)][0].astype(F32)
                    ysr[p, way, s - 1] = (ysr[p, way, s - 1].astype(F32) + term).astype(BF16)
                r_copy(p, way, s).start()

    def v_copy(way, n):
        return remote(
            vmid.at[way, n], vmid.at[way, n], v_send.at[way, n], v_recv.at[way, n], at_z(2 * way - 1)
        )

    def v_last(way, n):
        far = 1 - j // 2 if way == 0 else j // 2
        k = base[way] + n
        return remote(
            vmid.at[way, n], vfin.at[way, far], v_send.at[way, n], f_recv.at[way, far],
            at_z(-k if way == 0 else k),
        )

    def v_came(way, far):
        return remote(
            vmid.at[way, 0], vfin.at[way, far], v_send.at[way, 0], f_recv.at[way, far], at_z(2 * way - 1)
        )

    def r_finish(p):
        r_step(p, 5)
        total = tok[p, pl.ds(y, 1)][0].astype(F32)
        for way in (0, 1):
            total = total + ysr[p, way, y_steps(p)[way]].astype(F32)
        rs[p] = total
        for way in (0, 1):

            @pl.when(jnp.logical_not(hands_on(way)))
            def _():
                vmid[way, p] = rs[p, way].astype(BF16)
                v_copy(way, p).start()

    def v_step(n):
        for way in (0, 1):

            @pl.when(hands_on(way))
            def _():
                v_copy(way, n).wait_recv()
                vmid[way, n] = (rs[n, way] + vmid[way, n].astype(F32)).astype(BF16)
                v_last(way, n).start()

    for way in (0, 1):
        raw_first(way, 0).start()
        raw_first(way, 1).start()
    for k in (4, 3, 5, 2, 6, 1, 7):
        own_copy(k).start()
    place_own()
    for n in range(PAIRS):
        raw_relay(n)
    pack_own()
    raw_take(0)
    y_step(0, 1)
    raw_take(1)
    y_step(1, 1)
    y_step(0, 2)
    for d in (1, -1, 0):
        for k in range(1, NX):
            xo_copy(d, k).wait_recv()
    z_step(1)
    raw_take(2)
    y_step(2, 1)
    y_step(1, 2)
    y_step(0, 3)
    raw_take(3)
    y_step(3, 1)
    z_step(2)
    y_step(2, 2)
    y_step(1, 3)
    y_step(0, 4)
    y_step(3, 2)
    z_step(3)
    y_step(2, 3)
    y_step(1, 4)
    pack_pair(0)
    y_step(3, 3)
    z_step(4)
    y_step(2, 4)
    pack_pair(1)
    y_step(3, 4)
    for load in loads:
        load.wait()
    team_hidden(0, team)
    z_step(5)
    pack_pair(2)
    team_expert(0, team)
    pack_pair(3)
    z_step(6)
    beside = lax.rem(team + 3 - 2 * (j // 2), TEAMS)
    team_hidden(1, beside)
    pairs_hidden(2, 0)
    team_expert(1, beside)
    b_step(5)
    pairs_expert(2, 0)
    pairs_hidden(3, 2)
    b_step(4)
    pairs_expert(3, 2)
    combine_pair(0)
    r_step(0, 1)
    b_step(3)
    combine_pair(1)
    r_step(1, 1)
    r_step(0, 2)
    combine_pair(2)
    r_step(2, 1)
    r_step(1, 2)
    b_step(2)
    r_step(0, 3)
    combine_pair(3)
    r_step(3, 1)
    r_step(2, 2)
    r_step(1, 3)
    r_step(0, 4)
    b_step(1)
    r_step(3, 2)
    r_step(2, 3)
    r_step(1, 4)
    r_finish(0)
    finish_tree()
    r_step(3, 3)
    r_step(2, 4)
    r_finish(1)
    v_step(0)
    combine_own()
    for k in (4, 3, 5, 2, 6, 1, 7):
        last_copy(k).start()
    r_step(3, 4)
    r_finish(2)
    v_step(1)
    r_finish(3)
    v_step(2)
    v_step(3)
    total = tok_own[pl.ds(y, 1)][0].astype(F32)
    for k in range(1, ny):
        last_copy(k).wait_recv()
        total = total + ylast[k].astype(F32)
    for way in (0, 1):
        for far in (0, 1):
            v_came(way, far).wait_recv()
            total = total + vfin[way, far].astype(F32)
    out_ref[...] = total.astype(BF16)

    for k in range(1, ny):
        own_copy(k).wait_send()
        last_copy(k).wait_send()
    for way in (0, 1):
        for far in (0, 1):
            raw_first(way, far).wait_send()
        for n in range(PAIRS):

            @pl.when(hands_on(way))
            def _():
                raw_copy(way, n).wait_send()

            v_copy(way, n).wait_send()
        for p in range(PAIRS):
            for s in range(1, y_steps(p)[way] + 1):
                y_copy(p, way, s).wait_send()
                r_copy(p, way, s).wait_send()
    for k in range(1, NX):
        for d in (1, -1, 0):
            xo_copy(d, k).wait_send()
            co_copy(d, k).wait_send()
        for p in range(PAIRS):
            xz_copy(p, k).wait_send()
            cz_copy(p, k).wait_send()
    for n in range(TEAMS):
        h_copy(n).wait_send()
    for s in range(1, FAR + 1):
        for d in (1, 0):
            for way in (0, 1):
                _, _, i = place_of(way, s - 1)

                @pl.when(travels(i, s, d))
                def _():
                    z_copy(way, s, d, s - 1).wait_send()

                _, _, i = place_of(way, s)

                @pl.when(travels(i, s, d))
                def _():
                    b_copy(way, s, d, False).wait_send()


def per_device(ny, out_grad, expert_ids, gate_scores, saved_gate, saved_up, w_gate, w_up, w_down):
    feat = out_grad.shape[2]
    hid = w_down.shape[1]
    vmem = pl.BlockSpec(memory_space=pltpu.VMEM)
    hbm = pl.BlockSpec(memory_space=pl.ANY)
    saved_shape = (NX, NZ, Q, hid)
    rows = ny * Q
    chunk = TEAM * NX * Q

    def sems(*shape):
        return [pltpu.SemaphoreType.DMA(shape)] * 2

    out = pl.pallas_call(
        functools.partial(kernel, ny),
        out_shape=jax.ShapeDtypeStruct((Q, feat), BF16),
        in_specs=[vmem] * 3 + [hbm] * 5,
        out_specs=vmem,
        scratch_shapes=[
            pltpu.VMEM(saved_shape, BF16),
            pltpu.VMEM(saved_shape, BF16),
            pltpu.VMEM((feat, hid), BF16),
            pltpu.VMEM((feat, hid), BF16),
            pltpu.VMEM((hid, feat), BF16),
            pltpu.VMEM((Q, feat + META), BF16),
            pltpu.VMEM((2, PAIRS, Q, feat + META), BF16),
            pltpu.VMEM((ny, Q, feat), BF16),
            pltpu.VMEM((PAIRS, ny, 2, Q, feat), BF16),
            pltpu.VMEM((2, TEAMS * NX * Q, rows), BF16),
            pltpu.VMEM((PAIRS, 2, 2, NX * Q, rows), BF16),
            pltpu.VMEM((TEAMS, NX, Q, feat), BF16),
            pltpu.VMEM((PAIRS, NX, 2, Q, feat), BF16),
            pltpu.VMEM((NZ, TEAMS, NX, Q, feat), BF16),
            pltpu.VMEM((PAIRS, NX, 2, Q, feat), BF16),
            pltpu.VMEM((4, chunk, hid), F32),
            pltpu.VMEM((4, chunk, hid), F32),
            pltpu.VMEM((NZ, NX, Q, feat), BF16),
            pltpu.VMEM((PAIRS, NX, 2, Q, feat), BF16),
            pltpu.VMEM((2, NZ, TEAMS, NX, Q, feat), BF16),
            pltpu.VMEM((TEAMS, NX, Q, feat), BF16),
            pltpu.VMEM((TEAMS, NX, Q, feat), BF16),
            pltpu.VMEM((PAIRS, NX, 2, Q, feat), BF16),
            pltpu.VMEM((PAIRS, ny, 2, Q, feat), BF16),
            pltpu.VMEM((ny, Q, feat), BF16),
            pltpu.VMEM((PAIRS, 2, 5, 2, Q, feat), BF16),
            pltpu.VMEM((ny, Q, feat), BF16),
            pltpu.VMEM((PAIRS, 2, Q, feat), F32),
            pltpu.VMEM((2, PAIRS, Q, feat), BF16),
            pltpu.VMEM((2, 2, Q, feat), BF16),
            pltpu.SemaphoreType.DMA((5,)),
            *sems(2, 2 + PAIRS),
            *sems(ny),
            *sems(PAIRS, 2, 5),
            *sems(3, NX),
            *sems(PAIRS, NX),
            *sems(2, FAR + 1, 2),
            *sems(4),
            *sems(2, FAR + 1, 2),
            *sems(3, NX),
            *sems(PAIRS, NX),
            *sems(PAIRS, 2, 5),
            *sems(ny),
            *sems(2, PAIRS),
            *sems(2, 2),
        ],
        compiler_params=pltpu.CompilerParams(
            collective_id=0, has_side_effects=True, vmem_limit_bytes=56 * 1024 * 1024
        ),
        name="routed_backward",
    )(
        out_grad[0],
        expert_ids[0].T,
        gate_scores[0].T,
        saved_gate.reshape(saved_shape),
        saved_up.reshape(saved_shape),
        w_gate[0],
        w_up[0],
        w_down[0],
    )
    return out[None]


def solution(mesh):
    placed = (
        P("node", "group", "tp"),
        P("node", None, None),
        P("node", None, None),
        P(("group", "node"), None, None, None),
        P(("group", "node"), None, None, None),
        P(("group", "node"), "tp", None),
        P(("group", "node"), "tp", None),
        P(("group", "node"), None, "tp"),
    )
    return jax.shard_map(
        functools.partial(per_device, mesh.shape["group"]),
        mesh=mesh,
        in_specs=placed,
        out_specs=P("node", "group", "tp"),
        check_vma=False,
    )
```
